32 devices in a mesh: seq: 4 (over z), enc: 4 (over y, core), head: 2 (over x).
Axes of the slice: x: 2, y: 2, z: 4, core: 2. Of those that a mesh axis runs over, the one named last changes fastest.
Arguments:
- mel_frames: bfloat16 [8192, 128], P(('seq', 'enc')), may hold values from -6 to 6
- conv_weight: bfloat16 [384, 1280], replicated, may hold values from -0.3125 to 0.3125
- conv_bias: float32 [1280], replicated, may hold values from -3 to 3
- projector: bfloat16 [1280, 4, 512], P(None, None, 'head'), may hold values from -0.15625 to 0.15625
- seg_offsets: int32 [8], replicated, may hold values from 0 to 8191, as said below
- seg_lengths: int32 [8], replicated, may hold values from 1 to 1535, as said below
- text_embed: bfloat16 [8192, 2048], P('seq', ('enc', 'head')), may hold values from -6 to 6
- mix_taps: float32 [4, 2048], P(None, ('enc', 'head')), may hold values from -3 to 3
- input_map: bfloat16 [8192, 512], P('seq', 'enc'), may hold values from -1.796875 to 1.796875
- output_map: bfloat16 [8192, 512], P('seq', 'enc'), may hold values from -1.796875 to 1.796875
- step_size: float32 [32, 8192], P(('enc', 'head'), 'seq'), may hold values from 0 to 2, as said below
- decay_log: float32 [32], P(('enc', 'head')), may hold values from -6 to -2
- skip_gain: float32 [32], P(('enc', 'head')), may hold values from 0.5 to 1.5
Outputs:
- mixer_out: bfloat16 [8192, 2048], P('seq', ('enc', 'head'))
The draws below stay inside these ranges and needn't reach their ends.
Inputs may be any that keep to these rules, and one draw needn't show every extreme that they name: `seg_offsets`: offsets rise; owner k's two segments lie within positions k * 2048 to (k+1) * 2048 - 1 without intersection. Owner k's audio tokens are those of track indices within 256 of k * 1024 to (k+1) * 1024 - 1; in every draw some owner takes 256 tokens from each neighbour's share. `seg_lengths`: the lengths sum to 4096; an owner's two segments together hold between 512 and 1536 tokens. `step_size`: Positive.
All inputs are finite; a program needn't handle non-finite values.
Results may differ from the reference program's by a relative error of at most 0.006.
Values may be sent and summed in bfloat16 or wider, within the bound.
A program may use at most 64 MiB of HBM per device.

```python
import math
import jax
import jax.numpy as jnp
from jax import lax

MEL = 128
ENC_W = 1280
HDIM = 64
STATE = 128
SPAN = 128
L_DEV = 2048
HEADS = 32
INNER = 2048
GROUPS = 4
OWNERS = 4
SEQ_LEN = 8192
AUD_DEV = 1024
AUD = 4096
DRIFT = 256
N_ENC = 4


def layout(key):
    base_key = jax.random.fold_in(key, 7)
    drift_key = jax.random.fold_in(base_key, 1)
    first_key = jax.random.fold_in(base_key, 2)
    split_key = jax.random.fold_in(base_key, 4)
    inner_drift = jax.random.randint(drift_key, (OWNERS - 1,), -DRIFT, DRIFT + 1)
    big_owner = jax.random.randint(first_key, (), 1, OWNERS - 1)
    indices = jnp.arange(OWNERS - 1, dtype=jnp.int32)
    inner_drift = jnp.where(indices == big_owner, DRIFT, jnp.where(indices == big_owner - 1, -DRIFT, inner_drift))
    zero_one = jnp.zeros((1,), jnp.int32)
    drift_all = jnp.concatenate([zero_one, inner_drift.astype(jnp.int32), zero_one])
    audio_counts = AUD_DEV + drift_all[1:] - drift_all[:-1]
    text_counts = L_DEV - audio_counts
    raw_draws = jax.random.randint(split_key, (OWNERS, 3), 0, 1 << 20)
    owner_ids = jnp.arange(OWNERS, dtype=jnp.int32)
    is_last = owner_ids == OWNERS - 1
    forced = (owner_ids == big_owner) | is_last
    first_length = jnp.where(forced, audio_counts - 1, jnp.remainder(raw_draws[:, 0], audio_counts - 1) + 1)
    cut_one = jnp.remainder(raw_draws[:, 1], text_counts + 1)
    cut_two = jnp.where(is_last, text_counts, jnp.remainder(raw_draws[:, 2], text_counts + 1))
    low_cut = jnp.minimum(cut_one, cut_two)
    high_cut = jnp.maximum(cut_one, cut_two)
    block_base = owner_ids * L_DEV
    offset_first = block_base + low_cut
    offset_second = block_base + high_cut + first_length
    offsets = jnp.stack([offset_first, offset_second], axis=1).reshape(-1).astype(jnp.int32)
    lengths = jnp.stack([first_length, audio_counts - first_length], axis=1).reshape(-1).astype(jnp.int32)
    return (offsets, lengths)


def draw_seg_offsets(key, part):
    return layout(key)[0]


def draw_seg_lengths(key, part):
    return layout(key)[1]


def slow_heads(key):
    head_key = jax.random.fold_in(key, 11)
    share = 0.5
    return jax.random.uniform(head_key, (HEADS,), jnp.float32) < share


def draw_step_size(key, part):
    slow = slow_heads(key)
    rough_key = jax.random.fold_in(key, 23)
    owner_key = jax.random.fold_in(key, 29)
    rough = jnp.exp(jax.random.uniform(rough_key, (HEADS, SEQ_LEN), jnp.float32, math.log(0.5), math.log(2.0)))
    owner_scale = jnp.exp(jax.random.uniform(owner_key, (OWNERS,), jnp.float32, math.log(0.7), math.log(1.4)))
    per_place = jnp.repeat(owner_scale, L_DEV)
    head_scale = jnp.where(slow, 0.002, 0.5)
    return (head_scale[:, None] * rough * per_place[None, :]).astype(jnp.float32)


def draw_decay_log(key, part):
    slow = slow_heads(key)
    rate_key = jax.random.fold_in(key, 31)
    spread = jax.random.uniform(rate_key, (HEADS,), jnp.float32)
    slow_rate = math.log(0.003) + spread * (math.log(0.01) - math.log(0.003))
    fast_rate = math.log(0.03) + spread * (math.log(0.1) - math.log(0.03))
    return jnp.where(slow, slow_rate, fast_rate).astype(jnp.float32)


def level_of(rng, extent, pieces, low, top_value):
    loudness = 1.0
    for position, blocks in pieces:
        steps = jax.random.uniform(jax.random.fold_in(jax.random.fold_in(rng, 6), position), (blocks,), jnp.float32, low / len(pieces), top_value / len(pieces))
        loudness = loudness * jnp.repeat(jnp.exp(steps), extent[position] // blocks).reshape((-1,) + (1,) * (len(extent) - 1 - position))
    return loudness


def centred(stream_key, dims, scale, limit, shards=(), kind=jnp.bfloat16):
    values = jax.random.normal(stream_key, dims, jnp.float32) * scale
    if len(shards) > 0:
        values = level_of(stream_key, dims, shards, -0.22, 0.18) * values
    return jnp.clip(values, min=-limit, max=limit).astype(kind)


def setup_inputs(seed: int = 0) -> dict:
    key_list = jax.random.split(jax.random.key(seed), 14)
    mel_frames = centred(key_list[0], (2 * AUD, MEL), 1.0, 6.0, ((0, 16),))
    conv_weight = centred(key_list[1], (3 * MEL, ENC_W), (3 * MEL) ** -0.5, 0.3125)
    conv_bias = centred(key_list[2], (ENC_W,), 0.5, 3.0, (), jnp.float32)
    projector = centred(key_list[3], (ENC_W, N_ENC, INNER // N_ENC), ENC_W ** -0.5, 0.15625, ((2, 2),))
    seg_offsets = draw_seg_offsets(jax.random.fold_in(key_list[13], 71), 0)
    seg_lengths = draw_seg_lengths(jax.random.fold_in(key_list[13], 71), 0)
    text_embed = centred(key_list[6], (SEQ_LEN, INNER), 1.0, 6.0, ((0, 4), (1, 8)))
    mix_taps = centred(key_list[7], (4, INNER), 4 ** -0.5, 3.0, ((1, 8),), jnp.float32)
    input_map = centred(key_list[8], (SEQ_LEN, GROUPS * STATE), 0.3, 1.796875, ((0, 4), (1, 4)))
    output_map = centred(key_list[9], (SEQ_LEN, GROUPS * STATE), 0.3, 1.796875, ((0, 4), (1, 4)))
    step_size = draw_step_size(jax.random.fold_in(key_list[13], 71), 0)
    decay_log = draw_decay_log(jax.random.fold_in(key_list[13], 71), 0)
    skip_gain = jnp.clip(0.5 + 1.0 * jax.random.uniform(key_list[12], (HEADS,), jnp.float32) ** level_of(key_list[12], (HEADS,), ((0, 8),), -0.2, 0.2), 0.5, 1.5)
    return {"mel_frames": mel_frames, "conv_weight": conv_weight, "conv_bias": conv_bias, "projector": projector, "seg_offsets": seg_offsets, "seg_lengths": seg_lengths, "text_embed": text_embed, "mix_taps": mix_taps, "input_map": input_map, "output_map": output_map, "step_size": step_size, "decay_log": decay_log, "skip_gain": skip_gain}


highest = lax.Precision.HIGHEST
high_mode = lax.Precision.HIGH


def front_end(mel_frames, conv_weight, conv_bias, seg_lengths):
    seg_start = jnp.cumsum(seg_lengths) - seg_lengths
    frame_pairs = mel_frames.reshape(AUD, 2 * MEL)
    tokens = jnp.arange(AUD, dtype=jnp.int32)
    opening = jnp.any(tokens[:, None] == seg_start[None, :], axis=1)
    left_frames = jnp.concatenate([jnp.zeros((1, MEL), mel_frames.dtype), frame_pairs[:-1, MEL:]], axis=0)
    left_frames = jnp.where(opening[:, None], jnp.zeros_like(left_frames), left_frames)
    stacked = jnp.concatenate([left_frames, frame_pairs], axis=1)
    summed = jnp.dot(stacked, conv_weight, preferred_element_type=jnp.float32) + conv_bias
    return jax.nn.gelu(summed, approximate=False).astype(jnp.bfloat16)


def place_tokens(audio, text_embed, seg_offsets, seg_lengths):
    seg_start = jnp.cumsum(seg_lengths) - seg_lengths
    places = jnp.arange(SEQ_LEN, dtype=jnp.int32)
    segment = jnp.sum((places[:, None] >= seg_offsets[None, :]).astype(jnp.int32), axis=1) - 1
    clipped = jnp.maximum(segment, 0).astype(jnp.int32)
    within = places - seg_offsets[clipped]
    is_audio = (segment >= 0) & (within < seg_lengths[clipped])
    source = jnp.where(is_audio, seg_start[clipped] + within, 0).astype(jnp.int32)
    return jnp.where(is_audio[:, None], audio[source], text_embed)


def mix_conv(x_raw, tap_weights):
    row_count = x_raw.shape[0]
    padded = jnp.concatenate([jnp.zeros((3, x_raw.shape[1]), x_raw.dtype), x_raw], axis=0)
    summed = jnp.zeros(x_raw.shape, jnp.float32)
    for offset in range(4):
        summed = summed + padded[offset:offset + row_count].astype(jnp.float32) * tap_weights[offset]
    return jax.nn.silu(summed).astype(jnp.bfloat16)


def run_mixer(group_data):
    x_raw, tap_weights, b_rows, c_rows, step_rows, rate_logs, skips = group_data
    xconv = mix_conv(x_raw, tap_weights)
    head_count = step_rows.shape[0]
    blocks = SEQ_LEN // SPAN
    plain = xconv.reshape(blocks, SPAN, head_count, HDIM)
    b_all = b_rows.reshape(blocks, SPAN, STATE)
    c_all = c_rows.reshape(blocks, SPAN, STATE)
    step_sizes = step_rows.T.reshape(blocks, SPAN, head_count)
    rates = jnp.exp(rate_logs)
    lower_mask = (jnp.arange(SPAN)[:, None] >= jnp.arange(SPAN)[None, :])[:, :, None]

    def advance(state_now, block_data):
        plain_block, b_block, c_block, step_block = block_data
        value = plain_block.astype(jnp.float32)
        b_wide = b_block.astype(jnp.float32)
        c_wide = c_block.astype(jnp.float32)
        log_decay = -step_block * rates[None, :]
        running = jnp.cumsum(log_decay, axis=0)
        gap_logs = running[:, None, :] - running[None, :, :]
        decay_table = jnp.where(lower_mask, jnp.exp(jnp.where(lower_mask, gap_logs, 0.0)), 0.0)
        intersection = jnp.dot(c_block, b_block.T, preferred_element_type=jnp.float32)
        weight = (decay_table * intersection[:, :, None] * step_block[None, :, :]).astype(jnp.bfloat16)
        weight = lax.optimization_barrier(weight).astype(jnp.float32)
        inner_part = jnp.einsum("ijh,jhp->ihp", weight, value, precision=highest)
        inputs = value * step_block[:, :, None]
        carried = jnp.einsum("in,hpn->ihp", c_wide, state_now, precision=high_mode) * jnp.exp(running)[:, :, None]
        output = inner_part + carried + skips[None, :, None] * value
        tail_decay = jnp.exp(running[-1][None, :] - running)
        new_state = state_now * jnp.exp(running[-1])[:, None, None] + jnp.einsum(
            "jhp,jn->hpn", inputs * tail_decay[:, :, None], b_wide, precision=high_mode)
        return new_state, output

    initial = jnp.zeros((head_count, HDIM, STATE), jnp.float32)
    final_state, outputs = lax.scan(advance, initial, (plain, b_all, c_all, step_sizes))
    return outputs.reshape(SEQ_LEN, head_count * HDIM).astype(jnp.bfloat16)


def reference(mel_frames, conv_weight, conv_bias, projector, seg_offsets, seg_lengths, text_embed, mix_taps, input_map, output_map, step_size, decay_log, skip_gain):
    features = front_end(mel_frames, conv_weight, conv_bias, seg_lengths)
    audio = jnp.dot(features, projector.reshape(ENC_W, INNER), preferred_element_type=jnp.float32).astype(jnp.bfloat16)
    x_raw = place_tokens(audio, text_embed, seg_offsets, seg_lengths)
    group_width = INNER // GROUPS
    heads_group = HEADS // GROUPS
    grouped = (
        x_raw.reshape(SEQ_LEN, GROUPS, group_width).transpose(1, 0, 2),
        mix_taps.reshape(4, GROUPS, group_width).transpose(1, 0, 2),
        input_map.reshape(SEQ_LEN, GROUPS, STATE).transpose(1, 0, 2),
        output_map.reshape(SEQ_LEN, GROUPS, STATE).transpose(1, 0, 2),
        step_size.reshape(GROUPS, heads_group, SEQ_LEN),
        decay_log.reshape(GROUPS, heads_group),
        skip_gain.reshape(GROUPS, heads_group),
    )
    mixed = lax.map(run_mixer, grouped)
    return mixed.transpose(1, 0, 2).reshape(SEQ_LEN, INNER)
```

```python
import functools

import jax
import jax.numpy as jnp
from jax import lax
from jax.experimental import pallas as pl
from jax.experimental.pallas import tpu as pltpu
from jax.sharding import PartitionSpec as P

HDIM = 64
SPAN = 128
DRIFT = 256
TAIL = 16
PLACED = 256
FRONT = DRIFT + TAIL
MESH = pl.DeviceIdType.MESH
F32 = jnp.float32
BF16 = jnp.bfloat16


def kernel(
    owners,
    encs,
    seg_off,
    seg_len,
    mel,
    conv_w,
    bias,
    proj,
    text,
    taps,
    b_map,
    c_map,
    step,
    params,
    out,
    mel_f,
    edge,
    text_tail,
    feat,
    sent,
    wide,
    x_rows,
    xconv,
    step_s,
    run_s,
    weights,
    state,
    starts,
    before_s,
    y_s,
    mine,
    mine_total,
    states,
    totals,
    edge_sems,
    tail_sems,
    enc_send,
    enc_recv,
    front_send,
    front_recv,
    back_send,
    back_recv,
    state_send,
    state_recv,
    total_send,
    total_recv,
):
    s = lax.axis_index("seq")
    e = lax.axis_index("enc")
    frames = mel.shape[0]
    tiles = frames // 2
    share = encs * tiles
    rows, width = text.shape
    blocks = rows // SPAN
    heads = step.shape[0]
    halves = width // SPAN
    flat = s * encs + e
    segments = seg_off.shape[0]

    barrier = pltpu.get_barrier_semaphore()

    def greet(device):
        pl.semaphore_signal(barrier, inc=1, device_id=device, device_id_type=MESH)

    for j in range(1, encs):
        greet({"enc": lax.rem(e + j, encs)})

    @pl.when(s > 0)
    def _():
        for j in range(encs):
            greet({"seq": s - 1, "enc": j})

    @pl.when(s < owners - 1)
    def _():
        for j in range(encs):
            greet({"seq": s + 1, "enc": j})

    def greet_far(r, carry):
        @pl.when((r > s + 1) | (r < s - 1))
        def _():
            greet({"seq": r})

        return carry

    lax.fori_loop(0, owners, greet_far, 0)
    beside = (s > 0).astype(jnp.int32) + (s < owners - 1).astype(jnp.int32)
    pl.semaphore_wait(barrier, encs - 1 + beside * encs + owners - 1 - beside)

    edge_copy = pltpu.make_async_remote_copy(
        src_ref=mel.at[pl.ds(frames - TAIL, TAIL)],
        dst_ref=edge,
        send_sem=edge_sems.at[0],
        recv_sem=edge_sems.at[1],
        device_id={"seq": (flat + 1) // encs, "enc": lax.rem(e + 1, encs)},
        device_id_type=MESH,
    )
    tail_copy = pltpu.make_async_remote_copy(
        src_ref=text.at[pl.ds(rows - TAIL, TAIL)],
        dst_ref=text_tail,
        send_sem=tail_sems.at[0],
        recv_sem=tail_sems.at[1],
        device_id={"seq": s + 1},
        device_id_type=MESH,
    )

    @pl.when(flat < owners * encs - 1)
    def _():
        edge_copy.start()

    @pl.when(s < owners - 1)
    def _():
        tail_copy.start()

    step_s[...] = jnp.zeros_like(step_s)
    for c in range(blocks):
        step_s[c * 8 : c * 8 + heads, :] = step[:, c * SPAN : (c + 1) * SPAN]
    rate = params[0:8, 0:SPAN]
    logs = -(step_s[...].reshape(blocks, 8, SPAN) * rate[None]).reshape(blocks * 8, SPAN)
    row_ids = lax.broadcasted_iota(jnp.int32, (SPAN, SPAN), 0)
    lane_ids = lax.broadcasted_iota(jnp.int32, (SPAN, SPAN), 1)
    upper = (row_ids <= lane_ids).astype(F32)
    run_s[...] = jnp.dot(
        logs, upper, preferred_element_type=F32, precision=lax.Precision.HIGHEST
    )

    mel_f[8:, :] = mel[...].astype(F32)

    @pl.when(flat == 0)
    def _():
        mel_f[0:8, :] = jnp.zeros((8, mel.shape[1]), F32)

    tokens = flat * tiles + lax.broadcasted_iota(jnp.int32, (tiles, SPAN), 0)

    def opens(k, carry):
        begin, hit = carry
        return begin + seg_len[k], jnp.where(tokens == begin, 1, hit)

    _, opening = lax.fori_loop(
        0, segments, opens, (jnp.int32(0), jnp.zeros((tiles, SPAN), jnp.int32))
    )

    @pl.when(flat > 0)
    def _():
        edge_copy.wait_recv()
        mel_f[0:8, :] = edge[...].astype(F32)[TAIL - 8 :, :]

    left = jnp.where(opening > 0, 0.0, mel_f[pl.ds(7, tiles, stride=2), :])
    stacked = jnp.concatenate(
        [left, mel_f[pl.ds(8, tiles, stride=2), :], mel_f[pl.ds(9, tiles, stride=2), :]], axis=1
    ).astype(BF16)
    channels = conv_w.shape[1]
    for n in range(0, channels, 256):
        summed = (
            jnp.dot(stacked, conv_w[:, n : n + 256], preferred_element_type=F32)
            + bias[:, n : n + 256]
        )
        feat[:, n : n + 256] = (
            0.5 * summed * (1.0 + lax.erf(summed * (0.5**0.5)))
        ).astype(BF16)

    def enc_copy(b):
        return pltpu.make_async_remote_copy(
            src_ref=sent.at[b],
            dst_ref=wide.at[pl.ds(pl.multiple_of(FRONT + e * tiles, TAIL), tiles)],
            send_sem=enc_send.at[b],
            recv_sem=enc_recv.at[e],
            device_id={"enc": b},
            device_id_type=MESH,
        )

    fronts = {}
    backs = {}
    for t in range(encs):
        low = max(t * tiles, share - FRONT)
        if low < (t + 1) * tiles:
            fronts[t] = (low - t * tiles, (t + 1) * tiles - low, low - (share - FRONT))
        high = min((t + 1) * tiles, DRIFT)
        if high > t * tiles:
            backs[t] = (0, high - t * tiles, FRONT + share + t * tiles)

    def halo_copy(t, b, plan, send_sem, recv_sem, by):
        begin, count, place = plan[t]
        return pltpu.make_async_remote_copy(
            src_ref=sent.at[b, pl.ds(begin, count)],
            dst_ref=wide.at[pl.ds(place, count)],
            send_sem=send_sem.at[b],
            recv_sem=recv_sem.at[t],
            device_id={"seq": s + by, "enc": b},
            device_id_type=MESH,
        )

    def front_copy(t, b):
        return halo_copy(t, b, fronts, front_send, front_recv, 1)

    def back_copy(t, b):
        return halo_copy(t, b, backs, back_send, back_recv, -1)

    def project(j, carry):
        b = lax.rem(e + encs // 2 + j, encs)
        block = jnp.dot(feat[...], proj[b], preferred_element_type=F32).astype(BF16)
        sent[b] = block

        @pl.when(b != e)
        def _():
            enc_copy(b).start()

        @pl.when(b == e)
        def _():
            wide[pl.ds(pl.multiple_of(FRONT + e * tiles, TAIL), tiles), :] = block

        for t in fronts:

            @pl.when((e == t) & (s < owners - 1))
            def _(t=t):
                front_copy(t, b).start()

        for t in backs:

            @pl.when((e == t) & (s > 0))
            def _(t=t):
                back_copy(t, b).start()

        return carry

    lax.fori_loop(0, encs, project, 0)

    low_half = lane_ids < HDIM

    def block_rows(c):
        return pl.ds(pl.multiple_of(c * SPAN, SPAN), SPAN)

    def head_rows(c):
        return pl.ds(pl.multiple_of(c * 8, 8), 8)

    def spread(columns):
        return jnp.concatenate(
            [
                jnp.where(low_half, columns[:, 2 * i : 2 * i + 1], columns[:, 2 * i + 1 : 2 * i + 2])
                for i in range(halves)
            ],
            axis=1,
        )

    def make_weights(c, carry):
        both = lax.dot_general(
            c_map[block_rows(c), :],
            b_map[block_rows(c), :],
            (((1,), (1,)), ((), ())),
            preferred_element_type=F32,
        )
        run = run_s[head_rows(c), :]
        steps = step_s[head_rows(c), :]
        columns = jnp.transpose(run)
        for h in range(heads):
            gap = columns[:, h : h + 1] - run[h : h + 1, :]
            decay = jnp.exp(jnp.where(row_ids >= lane_ids, gap, -1e30))
            weights[c, h * SPAN : (h + 1) * SPAN, :] = (
                decay * both * steps[h : h + 1, :]
            ).astype(BF16)
        return carry

    lax.fori_loop(0, blocks, make_weights, 0)

    def start_of(last):
        return lax.fori_loop(0, last, lambda k, total: total + seg_len[k], jnp.int32(0))

    for j in range(1, encs):
        peer = lax.rem(e + j, encs)
        pltpu.make_async_remote_copy(
            src_ref=sent.at[peer],
            dst_ref=wide.at[pl.ds(pl.multiple_of(FRONT + peer * tiles, TAIL), tiles)],
            send_sem=enc_send.at[peer],
            recv_sem=enc_recv.at[peer],
            device_id={"enc": peer},
            device_id_type=MESH,
        ).wait_recv()

    @pl.when(s > 0)
    def _():
        tail_copy.wait_recv()
        for t in fronts:
            front_copy(t, 0).wait_recv()

    @pl.when(s < owners - 1)
    def _():
        for t in backs:
            back_copy(t, 0).wait_recv()

    @pl.when(s == 0)
    def _():
        wide[0:FRONT, :] = jnp.zeros((FRONT, width), BF16)
        text_tail[...] = jnp.zeros_like(text_tail)

    @pl.when(s == owners - 1)
    def _():
        wide[FRONT + share : FRONT + share + DRIFT, :] = jnp.zeros((DRIFT, width), BF16)

    held = wide.shape[0]
    spare = held - FRONT - share - DRIFT
    if spare:
        wide[held - spare :, :] = jnp.zeros((spare, width), BF16)

    def segment(k):
        return seg_off[k] - s * rows, seg_len[k], start_of(k) - s * share + FRONT

    def placed(first, count, parts, text_rows):
        ids = lax.broadcasted_iota(jnp.int32, (count, SPAN), 0)
        gaps = lax.broadcasted_iota(jnp.int32, (count, SPAN), 1) - ids
        here = first + ids
        shift = jnp.full((count, SPAN), -(1 << 30), jnp.int32)
        for offset, length, start in parts:
            inside = (here >= offset) & (here < offset + length)
            shift = jnp.where(inside, first - offset + start, shift)
        picks = jnp.concatenate(
            [
                jnp.where(gaps == shift - k, 1.0, 0.0).astype(BF16)
                for k in range(0, held, SPAN)
            ],
            axis=1,
        )
        audio = jnp.dot(picks, wide[...], preferred_element_type=F32)
        is_text = jnp.concatenate([shift] * halves, axis=1) < -(1 << 29)
        return jnp.where(is_text, text_rows, audio)

    own = [segment(2 * s), segment(2 * s + 1)]
    prior = 2 * lax.rem(s + owners - 1, owners)
    earlier = [segment(prior), segment(prior + 1)]
    past = placed(-TAIL, TAIL, earlier, text_tail[...].astype(F32))
    x_rows[0:8, :] = jnp.where(s > 0, past[TAIL - 8 :, :], 0.0)
    state[...] = jnp.zeros_like(state)

    def fill(c, carry):
        first = c * PLACED
        x_rows[pl.ds(pl.multiple_of(first + 8, 8), PLACED), :] = placed(
            first,
            PLACED,
            own,
            text[pl.ds(pl.multiple_of(first, PLACED), PLACED), :].astype(F32),
        )
        return carry

    lax.fori_loop(0, rows // PLACED, fill, 0)

    def place(c, before):
        first = c * SPAN
        near = x_rows[pl.ds(pl.multiple_of(first, 8), SPAN + 8), :]
        summed = near[5 : 5 + SPAN] * taps[0:1, :]
        for j in range(1, 4):
            summed = summed + near[5 + j : 5 + j + SPAN] * taps[j : j + 1, :]
        mixed = (summed / (1.0 + jnp.exp(-summed))).astype(BF16)
        xconv[block_rows(c), :] = mixed
        run = spread(jnp.transpose(run_s[head_rows(c), :]))
        steps = spread(jnp.transpose(step_s[head_rows(c), :]))
        last = run[SPAN - 1 : SPAN, :]
        inputs = (mixed.astype(F32) * (steps * jnp.exp(last - run))).astype(BF16)
        added = lax.dot_general(
            b_map[block_rows(c), :], inputs, (((0,), (0,)), ((), ())), preferred_element_type=F32
        )
        now = state[...]
        starts[c] = now.astype(BF16)
        before_s[c] = before
        state[...] = now * jnp.exp(last) + added
        return before + last

    total = lax.fori_loop(0, blocks, place, jnp.zeros((1, width), F32))

    mine[...] = state[...].astype(BF16)
    mine_total[...] = jnp.broadcast_to(total, mine_total.shape)

    def state_copies(to, slot):
        return (
            pltpu.make_async_remote_copy(
                src_ref=mine,
                dst_ref=states.at[slot],
                send_sem=state_send.at[to],
                recv_sem=state_recv.at[slot],
                device_id={"seq": to},
                device_id_type=MESH,
            ),
            pltpu.make_async_remote_copy(
                src_ref=mine_total,
                dst_ref=totals.at[slot],
                send_sem=total_send.at[to],
                recv_sem=total_recv.at[slot],
                device_id={"seq": to},
                device_id_type=MESH,
            ),
        )

    def send_state(to, carry):
        for copy in state_copies(to, s):
            copy.start()
        return carry

    lax.fori_loop(s + 1, owners, send_state, 0)

    skip = params[8:9, :]

    def inner(c, carry):
        mixed = xconv[block_rows(c), :]
        run = spread(jnp.transpose(run_s[head_rows(c), :]))
        wide_y = jnp.dot(weights[c], mixed, preferred_element_type=F32)
        within = jnp.concatenate(
            [
                jnp.where(
                    low_half,
                    wide_y[2 * i * SPAN : (2 * i + 1) * SPAN, i * SPAN : (i + 1) * SPAN],
                    wide_y[(2 * i + 1) * SPAN : (2 * i + 2) * SPAN, i * SPAN : (i + 1) * SPAN],
                )
                for i in range(halves)
            ],
            axis=1,
        )
        carried = jnp.dot(c_map[block_rows(c), :], starts[c], preferred_element_type=F32)
        y_s[block_rows(c), :] = within + carried * jnp.exp(run) + skip * mixed.astype(F32)
        return carry

    lax.fori_loop(0, blocks, inner, 0)

    state[...] = jnp.zeros_like(state)

    def join(r, carry):
        for copy in state_copies(s, r):
            copy.wait_recv()
        state[...] = state[...] * jnp.exp(totals[r][0:1, :]) + states[r].astype(F32)
        return carry

    lax.fori_loop(0, s, join, 0)
    incoming = state[...].astype(BF16)

    def finish(c, carry):
        run = spread(jnp.transpose(run_s[head_rows(c), :]))
        carried = jnp.dot(c_map[block_rows(c), :], incoming, preferred_element_type=F32)
        out[block_rows(c), :] = (
            y_s[block_rows(c), :] + carried * jnp.exp(before_s[c] + run)
        ).astype(BF16)
        return carry

    lax.fori_loop(0, blocks, finish, 0)

    @pl.when(flat < owners * encs - 1)
    def _():
        edge_copy.wait_send()

    @pl.when(s < owners - 1)
    def _():
        tail_copy.wait_send()

    for j in range(1, encs):
        enc_copy(lax.rem(e + j, encs)).wait_send()

    for b in range(encs):
        for t in fronts:

            @pl.when((e == t) & (s < owners - 1))
            def _(t=t, b=b):
                front_copy(t, b).wait_send()

        for t in backs:

            @pl.when((e == t) & (s > 0))
            def _(t=t, b=b):
                back_copy(t, b).wait_send()

    def sent_state(to, carry):
        for copy in state_copies(to, s):
            copy.wait_send()
        return carry

    lax.fori_loop(s + 1, owners, sent_state, 0)


def shards(
    mel_frames,
    conv_weight,
    conv_bias,
    projector,
    seg_offsets,
    seg_lengths,
    text_embed,
    mix_taps,
    input_map,
    output_map,
    step_size,
    decay_log,
    skip_gain,
):
    owners = lax.axis_size("seq")
    encs = lax.axis_size("enc")
    frames, mels = mel_frames.shape
    tiles = frames // 2
    channels = conv_weight.shape[1]
    rows, width = text_embed.shape
    heads = step_size.shape[0]
    blocks = rows // SPAN
    states = input_map.shape[1]
    held = -(-(FRONT + encs * tiles + DRIFT) // SPAN) * SPAN
    rates = jnp.zeros((8, width), F32).at[:heads].set(
        jnp.broadcast_to(jnp.exp(decay_log)[:, None], (heads, width))
    )
    skips = jnp.broadcast_to(
        jnp.broadcast_to(skip_gain[:, None], (heads, HDIM)).reshape(1, width), (8, width)
    )
    params = jnp.concatenate([rates, skips], axis=0)
    vmem = pl.BlockSpec(memory_space=pltpu.VMEM)
    smem = pl.BlockSpec(memory_space=pltpu.SMEM)
    dma = pltpu.SemaphoreType.DMA
    return pl.pallas_call(
        functools.partial(kernel, owners, encs),
        out_shape=jax.ShapeDtypeStruct((rows, width), BF16),
        in_specs=[smem, smem] + [vmem] * 10,
        out_specs=vmem,
        scratch_shapes=[
            pltpu.VMEM((8 + frames, mels), F32),
            pltpu.VMEM((TAIL, mels), BF16),
            pltpu.VMEM((TAIL, width), BF16),
            pltpu.VMEM((tiles, channels), BF16),
            pltpu.VMEM((encs, tiles, width), BF16),
            pltpu.VMEM((held, width), BF16),
            pltpu.VMEM((rows + 8, width), F32),
            pltpu.VMEM((rows, width), BF16),
            pltpu.VMEM((blocks * 8, SPAN), F32),
            pltpu.VMEM((blocks * 8, SPAN), F32),
            pltpu.VMEM((blocks, heads * SPAN, SPAN), BF16),
            pltpu.VMEM((states, width), F32),
            pltpu.VMEM((blocks, states, width), BF16),
            pltpu.VMEM((blocks, 1, width), F32),
            pltpu.VMEM((rows, width), F32),
            pltpu.VMEM((states, width), BF16),
            pltpu.VMEM((8, width), F32),
            pltpu.VMEM((owners, states, width), BF16),
            pltpu.VMEM((owners, 8, width), F32),
            dma((2,)),
            dma((2,)),
            dma((encs,)),
            dma((encs,)),
            dma((encs,)),
            dma((encs,)),
            dma((encs,)),
            dma((encs,)),
            dma((owners,)),
            dma((owners,)),
            dma((owners,)),
            dma((owners,)),
        ],
        compiler_params=pltpu.CompilerParams(
            collective_id=0, has_side_effects=True, vmem_limit_bytes=48 * 1024 * 1024
        ),
    )(
        seg_offsets,
        seg_lengths,
        mel_frames,
        conv_weight,
        conv_bias[None, :],
        jnp.transpose(projector, (1, 0, 2)),
        text_embed,
        mix_taps,
        input_map,
        output_map,
        step_size,
        params,
    )


def solution(mesh):
    return jax.shard_map(
        shards,
        mesh=mesh,
        in_specs=(
            P(("seq", "enc"), None),
            P(),
            P(),
            P(None, None, "head"),
            P(),
            P(),
            P("seq", ("enc", "head")),
            P(None, ("enc", "head")),
            P("seq", "enc"),
            P("seq", "enc"),
            P(("enc", "head"), "seq"),
            P(("enc", "head")),
            P(("enc", "head")),
        ),
        out_specs=P("seq", ("enc", "head")),
        check_vma=False,
    )
```

```python
import functools

import jax
import jax.numpy as jnp
from jax import lax
from jax.experimental import pallas as pl
from jax.experimental.pallas import tpu as pltpu
from jax.sharding import PartitionSpec as P

HDIM = 64
SPAN = 128
DRIFT = 256
TAIL = 16
PLACED = 256
FRONT = DRIFT + TAIL
MESH = pl.DeviceIdType.MESH
F32 = jnp.float32
BF16 = jnp.bfloat16


def kernel(
    owners,
    encs,
    seg_off,
    seg_len,
    mel,
    conv_w,
    bias,
    proj,
    text,
    taps,
    b_map,
    c_map,
    step,
    decay_log,
    skip_gain,
    out,
    mel_f,
    edge,
    text_tail,
    feat,
    sent,
    wide,
    x_rows,
    xconv,
    step_s,
    run_s,
    weights,
    grown,
    tails,
    state,
    starts,
    before_s,
    lasts,
    y_s,
    mine,
    mine_total,
    states,
    totals,
    edge_sems,
    tail_sems,
    enc_send,
    enc_recv,
    front_send,
    front_recv,
    back_send,
    back_recv,
    state_send,
    state_recv,
    total_send,
    total_recv,
):
    s = lax.axis_index("seq")
    e = lax.axis_index("enc")
    frames = mel.shape[0]
    tiles = frames // 2
    share = encs * tiles
    rows, width = text.shape
    blocks = rows // SPAN
    heads = step.shape[0]
    halves = width // SPAN
    flat = s * encs + e
    segments = seg_off.shape[0]

    barrier = pltpu.get_barrier_semaphore()

    def greet(device):
        pl.semaphore_signal(barrier, inc=1, device_id=device, device_id_type=MESH)

    for j in range(1, encs):
        greet({"enc": lax.rem(e + j, encs)})

    @pl.when(s > 0)
    def _():
        for j in range(encs):
            greet({"seq": s - 1, "enc": j})

    @pl.when(s < owners - 1)
    def _():
        for j in range(encs):
            greet({"seq": s + 1, "enc": j})

    def greet_far(r, carry):
        @pl.when((r > s + 1) | (r < s - 1))
        def _():
            greet({"seq": r})

        return carry

    lax.fori_loop(0, owners, greet_far, 0)
    beside = (s > 0).astype(jnp.int32) + (s < owners - 1).astype(jnp.int32)
    pl.semaphore_wait(barrier, encs - 1 + beside * encs + owners - 1 - beside)

    edge_copy = pltpu.make_async_remote_copy(
        src_ref=mel.at[pl.ds(frames - TAIL, TAIL)],
        dst_ref=edge,
        send_sem=edge_sems.at[0],
        recv_sem=edge_sems.at[1],
        device_id={"seq": (flat + 1) // encs, "enc": lax.rem(e + 1, encs)},
        device_id_type=MESH,
    )
    tail_copy = pltpu.make_async_remote_copy(
        src_ref=text.at[pl.ds(rows - TAIL, TAIL)],
        dst_ref=text_tail,
        send_sem=tail_sems.at[0],
        recv_sem=tail_sems.at[1],
        device_id={"seq": s + 1},
        device_id_type=MESH,
    )

    @pl.when(flat < owners * encs - 1)
    def _():
        edge_copy.start()

    @pl.when(s < owners - 1)
    def _():
        tail_copy.start()

    step_s[...] = jnp.zeros_like(step_s)
    for c in range(blocks):
        step_s[c * 8 : c * 8 + heads, :] = step[:, c * SPAN : (c + 1) * SPAN]
    head_ids = lax.broadcasted_iota(jnp.int32, (8, SPAN), 0)
    rate = jnp.zeros((8, SPAN), F32)
    for h in range(heads):
        rate = jnp.where(head_ids == h, jnp.exp(jnp.full((8, SPAN), decay_log[h], F32)), rate)
    logs = -(step_s[...].reshape(blocks, 8, SPAN) * rate[None]).reshape(blocks * 8, SPAN)
    row_ids = lax.broadcasted_iota(jnp.int32, (SPAN, SPAN), 0)
    lane_ids = lax.broadcasted_iota(jnp.int32, (SPAN, SPAN), 1)
    upper = (row_ids <= lane_ids).astype(F32)
    run_s[...] = jnp.dot(
        logs, upper, preferred_element_type=F32, precision=lax.Precision.HIGHEST
    )

    mel_f[8:, :] = mel[...].astype(F32)

    @pl.when(flat == 0)
    def _():
        mel_f[0:8, :] = jnp.zeros((8, mel.shape[1]), F32)

    tokens = flat * tiles + lax.broadcasted_iota(jnp.int32, (tiles, SPAN), 0)

    def opens(k, carry):
        begin, hit = carry
        return begin + seg_len[k], jnp.where(tokens == begin, 1, hit)

    _, opening = lax.fori_loop(
        0, segments, opens, (jnp.int32(0), jnp.zeros((tiles, SPAN), jnp.int32))
    )

    @pl.when(flat > 0)
    def _():
        edge_copy.wait_recv()
        mel_f[0:8, :] = edge[...].astype(F32)[TAIL - 8 :, :]

    left = jnp.where(opening > 0, 0.0, mel_f[pl.ds(7, tiles, stride=2), :])
    stacked = jnp.concatenate(
        [left, mel_f[pl.ds(8, tiles, stride=2), :], mel_f[pl.ds(9, tiles, stride=2), :]], axis=1
    ).astype(BF16)
    channels = conv_w.shape[1]
    for n in range(0, channels, 256):
        summed = (
            jnp.dot(stacked, conv_w[:, n : n + 256], preferred_element_type=F32)
            + jnp.concatenate(
                [bias[k : k + 1, :] for k in range(n // SPAN, (n + 256) // SPAN)], axis=1
            )
        )
        feat[:, n : n + 256] = (
            0.5 * summed * (1.0 + lax.erf(summed * (0.5**0.5)))
        ).astype(BF16)

    def enc_copy(b):
        return pltpu.make_async_remote_copy(
            src_ref=sent.at[b],
            dst_ref=wide.at[pl.ds(pl.multiple_of(FRONT + e * tiles, TAIL), tiles)],
            send_sem=enc_send.at[b],
            recv_sem=enc_recv.at[e],
            device_id={"enc": b},
            device_id_type=MESH,
        )

    fronts = {}
    backs = {}
    for t in range(encs):
        low = max(t * tiles, share - FRONT)
        if low < (t + 1) * tiles:
            fronts[t] = (low - t * tiles, (t + 1) * tiles - low, low - (share - FRONT))
        high = min((t + 1) * tiles, DRIFT)
        if high > t * tiles:
            backs[t] = (0, high - t * tiles, FRONT + share + t * tiles)

    def halo_copy(t, b, plan, send_sem, recv_sem, by):
        begin, count, place = plan[t]
        return pltpu.make_async_remote_copy(
            src_ref=sent.at[b, pl.ds(begin, count)],
            dst_ref=wide.at[pl.ds(place, count)],
            send_sem=send_sem.at[b],
            recv_sem=recv_sem.at[t],
            device_id={"seq": s + by, "enc": b},
            device_id_type=MESH,
        )

    def front_copy(t, b):
        return halo_copy(t, b, fronts, front_send, front_recv, 1)

    def back_copy(t, b):
        return halo_copy(t, b, backs, back_send, back_recv, -1)

    def project(j, carry):
        b = lax.rem(e + encs // 2 + j, encs)
        block = jnp.dot(feat[...], proj[b], preferred_element_type=F32).astype(BF16)
        sent[b] = block

        @pl.when(b != e)
        def _():
            enc_copy(b).start()

        @pl.when(b == e)
        def _():
            wide[pl.ds(pl.multiple_of(FRONT + e * tiles, TAIL), tiles), :] = block

        for t in fronts:

            @pl.when((e == t) & (s < owners - 1))
            def _(t=t):
                front_copy(t, b).start()

        for t in backs:

            @pl.when((e == t) & (s > 0))
            def _(t=t):
                back_copy(t, b).start()

        return carry

    lax.fori_loop(0, encs, project, 0)

    low_half = lane_ids < HDIM

    def block_rows(c):
        return pl.ds(pl.multiple_of(c * SPAN, SPAN), SPAN)

    def head_rows(c):
        return pl.ds(pl.multiple_of(c * 8, 8), 8)

    def spread(columns):
        return jnp.concatenate(
            [
                jnp.where(low_half, columns[:, 2 * i : 2 * i + 1], columns[:, 2 * i + 1 : 2 * i + 2])
                for i in range(halves)
            ],
            axis=1,
        )

    def make_weights(c, carry):
        both = lax.dot_general(
            c_map[block_rows(c), :],
            b_map[block_rows(c), :],
            (((1,), (1,)), ((), ())),
            preferred_element_type=F32,
        )
        run = run_s[head_rows(c), :]
        steps = step_s[head_rows(c), :]
        columns = jnp.transpose(run)
        for h in range(heads):
            gap = columns[:, h : h + 1] - run[h : h + 1, :]
            decay = jnp.exp(jnp.where(row_ids >= lane_ids, gap, -1e30))
            weights[c, h * SPAN : (h + 1) * SPAN, :] = (
                decay * both * steps[h : h + 1, :]
            ).astype(BF16)
        run_wide = spread(columns)
        last = run_wide[SPAN - 1 : SPAN, :]
        grown[block_rows(c), :] = jnp.exp(run_wide)
        tails[block_rows(c), :] = spread(jnp.transpose(steps)) * jnp.exp(last - run_wide)
        lasts[c] = last
        return carry

    lax.fori_loop(0, blocks, make_weights, 0, unroll=2)

    def start_of(last):
        return lax.fori_loop(0, last, lambda k, total: total + seg_len[k], jnp.int32(0))

    for j in range(1, encs):
        peer = lax.rem(e + j, encs)
        pltpu.make_async_remote_copy(
            src_ref=sent.at[peer],
            dst_ref=wide.at[pl.ds(pl.multiple_of(FRONT + peer * tiles, TAIL), tiles)],
            send_sem=enc_send.at[peer],
            recv_sem=enc_recv.at[peer],
            device_id={"enc": peer},
            device_id_type=MESH,
        ).wait_recv()

    @pl.when(s > 0)
    def _():
        tail_copy.wait_recv()
        for t in fronts:
            front_copy(t, 0).wait_recv()

    @pl.when(s < owners - 1)
    def _():
        for t in backs:
            back_copy(t, 0).wait_recv()

    @pl.when(s == 0)
    def _():
        wide[0:FRONT, :] = jnp.zeros((FRONT, width), BF16)
        text_tail[...] = jnp.zeros_like(text_tail)

    @pl.when(s == owners - 1)
    def _():
        wide[FRONT + share : FRONT + share + DRIFT, :] = jnp.zeros((DRIFT, width), BF16)

    held = wide.shape[0]
    spare = held - FRONT - share - DRIFT
    if spare:
        wide[held - spare :, :] = jnp.zeros((spare, width), BF16)

    def segment(k):
        return seg_off[k] - s * rows, seg_len[k], start_of(k) - s * share + FRONT

    def placed(first, count, parts, text_rows):
        ids = lax.broadcasted_iota(jnp.int32, (count, SPAN), 0)
        gaps = lax.broadcasted_iota(jnp.int32, (count, SPAN), 1) - ids
        here = first + ids
        shift = jnp.full((count, SPAN), -(1 << 30), jnp.int32)
        for offset, length, start in parts:
            inside = (here >= offset) & (here < offset + length)
            shift = jnp.where(inside, first - offset + start, shift)
        picks = jnp.concatenate(
            [
                jnp.where(gaps == shift - k, 1.0, 0.0).astype(BF16)
                for k in range(0, held, SPAN)
            ],
            axis=1,
        )
        audio = jnp.dot(picks, wide[...], preferred_element_type=F32)
        is_text = jnp.concatenate([shift] * halves, axis=1) < -(1 << 29)
        return jnp.where(is_text, text_rows, audio)

    own = [segment(2 * s), segment(2 * s + 1)]
    prior = 2 * lax.rem(s + owners - 1, owners)
    earlier = [segment(prior), segment(prior + 1)]
    past = placed(-TAIL, TAIL, earlier, text_tail[...].astype(F32))
    x_rows[0:8, :] = jnp.where(s > 0, past[TAIL - 8 :, :], 0.0)
    state[...] = jnp.zeros_like(state)

    def fill(c, carry):
        first = c * PLACED
        x_rows[pl.ds(pl.multiple_of(first + 8, 8), PLACED), :] = placed(
            first,
            PLACED,
            own,
            text[pl.ds(pl.multiple_of(first, PLACED), PLACED), :].astype(F32),
        )
        return carry

    lax.fori_loop(0, rows // PLACED, fill, 0)

    def place(c, before):
        first = c * SPAN
        near = x_rows[pl.ds(pl.multiple_of(first, 8), SPAN + 8), :]
        summed = near[5 : 5 + SPAN] * taps[0:1, :]
        for j in range(1, 4):
            summed = summed + near[5 + j : 5 + j + SPAN] * taps[j : j + 1, :]
        mixed = (summed / (1.0 + jnp.exp(-summed))).astype(BF16)
        xconv[block_rows(c), :] = mixed
        last = lasts[c]
        inputs = (mixed.astype(F32) * tails[block_rows(c), :]).astype(BF16)
        added = lax.dot_general(
            b_map[block_rows(c), :], inputs, (((0,), (0,)), ((), ())), preferred_element_type=F32
        )
        now = state[...]
        starts[c] = now.astype(BF16)
        before_s[c] = jnp.exp(before)
        state[...] = now * jnp.exp(last) + added
        return before + last

    total = lax.fori_loop(0, blocks, place, jnp.zeros((1, width), F32), unroll=2)

    mine[...] = state[...].astype(BF16)
    mine_total[...] = jnp.broadcast_to(total, mine_total.shape)

    def state_copies(to, slot):
        return (
            pltpu.make_async_remote_copy(
                src_ref=mine,
                dst_ref=states.at[slot],
                send_sem=state_send.at[to],
                recv_sem=state_recv.at[slot],
                device_id={"seq": to},
                device_id_type=MESH,
            ),
            pltpu.make_async_remote_copy(
                src_ref=mine_total,
                dst_ref=totals.at[slot],
                send_sem=total_send.at[to],
                recv_sem=total_recv.at[slot],
                device_id={"seq": to},
                device_id_type=MESH,
            ),
        )

    def send_state(to, carry):
        for copy in state_copies(to, s):
            copy.start()
        return carry

    lax.fori_loop(s + 1, owners, send_state, 0)

    skip = jnp.concatenate(
        [
            jnp.where(low_half[0:1, :], skip_gain[2 * i], skip_gain[2 * i + 1])
            for i in range(halves)
        ],
        axis=1,
    )

    def inner(c, carry):
        mixed = xconv[block_rows(c), :]
        wide_y = jnp.dot(weights[c], mixed, preferred_element_type=F32)
        within = jnp.concatenate(
            [
                jnp.where(
                    low_half,
                    wide_y[2 * i * SPAN : (2 * i + 1) * SPAN, i * SPAN : (i + 1) * SPAN],
                    wide_y[(2 * i + 1) * SPAN : (2 * i + 2) * SPAN, i * SPAN : (i + 1) * SPAN],
                )
                for i in range(halves)
            ],
            axis=1,
        )
        carried = jnp.dot(c_map[block_rows(c), :], starts[c], preferred_element_type=F32)
        y_s[block_rows(c), :] = (
            within + carried * grown[block_rows(c), :] + skip * mixed.astype(F32)
        )
        return carry

    lax.fori_loop(0, blocks, inner, 0, unroll=2)

    state[...] = jnp.zeros_like(state)

    def join(r, carry):
        for copy in state_copies(s, r):
            copy.wait_recv()
        state[...] = state[...] * jnp.exp(totals[r][0:1, :]) + states[r].astype(F32)
        return carry

    lax.fori_loop(0, s, join, 0)
    incoming = state[...].astype(BF16)

    def finish(c, carry):
        carried = jnp.dot(c_map[block_rows(c), :], incoming, preferred_element_type=F32)
        out[block_rows(c), :] = (
            y_s[block_rows(c), :] + carried * before_s[c] * grown[block_rows(c), :]
        ).astype(BF16)
        return carry

    lax.fori_loop(0, blocks, finish, 0, unroll=4)

    @pl.when(flat < owners * encs - 1)
    def _():
        edge_copy.wait_send()

    @pl.when(s < owners - 1)
    def _():
        tail_copy.wait_send()

    for j in range(1, encs):
        enc_copy(lax.rem(e + j, encs)).wait_send()

    for b in range(encs):
        for t in fronts:

            @pl.when((e == t) & (s < owners - 1))
            def _(t=t, b=b):
                front_copy(t, b).wait_send()

        for t in backs:

            @pl.when((e == t) & (s > 0))
            def _(t=t, b=b):
                back_copy(t, b).wait_send()

    def sent_state(to, carry):
        for copy in state_copies(to, s):
            copy.wait_send()
        return carry

    lax.fori_loop(s + 1, owners, sent_state, 0)


def shards(
    mel_frames,
    conv_weight,
    conv_bias,
    projector,
    seg_offsets,
    seg_lengths,
    text_embed,
    mix_taps,
    input_map,
    output_map,
    step_size,
    decay_log,
    skip_gain,
):
    owners = lax.axis_size("seq")
    encs = lax.axis_size("enc")
    frames, mels = mel_frames.shape
    tiles = frames // 2
    channels = conv_weight.shape[1]
    rows, width = text_embed.shape
    heads = step_size.shape[0]
    blocks = rows // SPAN
    states = input_map.shape[1]
    held = -(-(FRONT + encs * tiles + DRIFT) // SPAN) * SPAN
    vmem = pl.BlockSpec(memory_space=pltpu.VMEM)
    smem = pl.BlockSpec(memory_space=pltpu.SMEM)
    dma = pltpu.SemaphoreType.DMA
    return pl.pallas_call(
        functools.partial(kernel, owners, encs),
        out_shape=jax.ShapeDtypeStruct((rows, width), BF16),
        in_specs=[smem, smem] + [vmem] * 9 + [smem, smem],
        out_specs=vmem,
        scratch_shapes=[
            pltpu.VMEM((8 + frames, mels), F32),
            pltpu.VMEM((TAIL, mels), BF16),
            pltpu.VMEM((TAIL, width), BF16),
            pltpu.VMEM((tiles, channels), BF16),
            pltpu.VMEM((encs, tiles, width), BF16),
            pltpu.VMEM((held, width), BF16),
            pltpu.VMEM((rows + 8, width), F32),
            pltpu.VMEM((rows, width), BF16),
            pltpu.VMEM((blocks * 8, SPAN), F32),
            pltpu.VMEM((blocks * 8, SPAN), F32),
            pltpu.VMEM((blocks, heads * SPAN, SPAN), BF16),
            pltpu.VMEM((rows, width), F32),
            pltpu.VMEM((rows, width), F32),
            pltpu.VMEM((states, width), F32),
            pltpu.VMEM((blocks, states, width), BF16),
            pltpu.VMEM((blocks, 1, width), F32),
            pltpu.VMEM((blocks, 1, width), F32),
            pltpu.VMEM((rows, width), F32),
            pltpu.VMEM((states, width), BF16),
            pltpu.VMEM((8, width), F32),
            pltpu.VMEM((owners, states, width), BF16),
            pltpu.VMEM((owners, 8, width), F32),
            dma((2,)),
            dma((2,)),
            dma((encs,)),
            dma((encs,)),
            dma((encs,)),
            dma((encs,)),
            dma((encs,)),
            dma((encs,)),
            dma((owners,)),
            dma((owners,)),
            dma((owners,)),
            dma((owners,)),
        ],
        compiler_params=pltpu.CompilerParams(
            collective_id=0, has_side_effects=True, vmem_limit_bytes=48 * 1024 * 1024
        ),
    )(
        seg_offsets,
        seg_lengths,
        mel_frames,
        conv_weight,
        conv_bias.reshape(channels // SPAN, SPAN),
        jnp.transpose(projector, (1, 0, 2)),
        text_embed,
        mix_taps,
        input_map,
        output_map,
        step_size,
        decay_log,
        skip_gain,
    )


def solution(mesh):
    return jax.shard_map(
        shards,
        mesh=mesh,
        in_specs=(
            P(("seq", "enc"), None),
            P(),
            P(),
            P(None, None, "head"),
            P(),
            P(),
            P("seq", ("enc", "head")),
            P(None, ("enc", "head")),
            P("seq", "enc"),
            P("seq", "enc"),
            P(("enc", "head"), "seq"),
            P(("enc", "head")),
            P(("enc", "head")),
        ),
        out_specs=P("seq", ("enc", "head")),
        check_vma=False,
    )
```

```python
import functools

import jax
import jax.numpy as jnp
from jax import lax
from jax.experimental import pallas as pl
from jax.experimental.pallas import tpu as pltpu
from jax.sharding import PartitionSpec as P

HDIM = 64
SPAN = 128
DRIFT = 256
TAIL = 16
PLACED = 256
FRONT = DRIFT + TAIL
MESH = pl.DeviceIdType.MESH
F32 = jnp.float32
BF16 = jnp.bfloat16


def kernel(
    owners,
    encs,
    seg_off,
    seg_len,
    mel,
    conv_w,
    bias,
    proj,
    text,
    taps,
    b_map,
    c_map,
    step,
    decay_log,
    skip_gain,
    out,
    mel_f,
    edge,
    text_tail,
    feat,
    sent,
    wide,
    x_rows,
    xconv,
    step_s,
    run_s,
    weights,
    grown,
    tails,
    state,
    starts,
    before_s,
    lasts,
    y_s,
    mine,
    mine_total,
    states,
    totals,
    edge_sems,
    tail_sems,
    enc_send,
    enc_recv,
    front_send,
    front_recv,
    back_send,
    back_recv,
    state_send,
    state_recv,
    total_send,
    total_recv,
):
    s = lax.axis_index("seq")
    e = lax.axis_index("enc")
    frames = mel.shape[0]
    tiles = frames // 2
    share = encs * tiles
    rows, width = text.shape
    blocks = rows // SPAN
    heads = step.shape[0]
    halves = width // SPAN
    flat = s * encs + e
    segments = seg_off.shape[0]

    barrier = pltpu.get_barrier_semaphore()

    def greet(device):
        pl.semaphore_signal(barrier, inc=1, device_id=device, device_id_type=MESH)

    for j in range(1, encs):
        greet({"enc": lax.rem(e + j, encs)})

    @pl.when(s > 0)
    def _():
        for j in range(encs):
            greet({"seq": s - 1, "enc": j})

    @pl.when(s < owners - 1)
    def _():
        for j in range(encs):
            greet({"seq": s + 1, "enc": j})

    def greet_far(r, carry):
        @pl.when((r > s + 1) | (r < s - 1))
        def _():
            greet({"seq": r})

        return carry

    lax.fori_loop(0, owners, greet_far, 0)
    beside = (s > 0).astype(jnp.int32) + (s < owners - 1).astype(jnp.int32)
    pl.semaphore_wait(barrier, encs - 1 + beside * encs + owners - 1 - beside)

    edge_copy = pltpu.make_async_remote_copy(
        src_ref=mel.at[pl.ds(frames - TAIL, TAIL)],
        dst_ref=edge,
        send_sem=edge_sems.at[0],
        recv_sem=edge_sems.at[1],
        device_id={"seq": (flat + 1) // encs, "enc": lax.rem(e + 1, encs)},
        device_id_type=MESH,
    )
    tail_copy = pltpu.make_async_remote_copy(
        src_ref=text.at[pl.ds(rows - TAIL, TAIL)],
        dst_ref=text_tail,
        send_sem=tail_sems.at[0],
        recv_sem=tail_sems.at[1],
        device_id={"seq": s + 1},
        device_id_type=MESH,
    )

    @pl.when(flat < owners * encs - 1)
    def _():
        edge_copy.start()

    @pl.when(s < owners - 1)
    def _():
        tail_copy.start()

    step_s[...] = jnp.zeros_like(step_s)
    for c in range(blocks):
        step_s[c * 8 : c * 8 + heads, :] = step[:, c * SPAN : (c + 1) * SPAN]
    head_ids = lax.broadcasted_iota(jnp.int32, (8, SPAN), 0)
    rate = jnp.zeros((8, SPAN), F32)
    for h in range(heads):
        rate = jnp.where(head_ids == h, jnp.exp(jnp.full((8, SPAN), decay_log[h], F32)), rate)
    logs = -(step_s[...].reshape(blocks, 8, SPAN) * rate[None]).reshape(blocks * 8, SPAN)
    row_ids = lax.broadcasted_iota(jnp.int32, (SPAN, SPAN), 0)
    lane_ids = lax.broadcasted_iota(jnp.int32, (SPAN, SPAN), 1)
    upper = (row_ids <= lane_ids).astype(F32)
    run_s[...] = jnp.dot(
        logs, upper, preferred_element_type=F32, precision=lax.Precision.HIGHEST
    )

    mel_f[8:, :] = mel[...].astype(F32)

    @pl.when(flat == 0)
    def _():
        mel_f[0:8, :] = jnp.zeros((8, mel.shape[1]), F32)

    tokens = flat * tiles + lax.broadcasted_iota(jnp.int32, (tiles, SPAN), 0)

    def opens(k, carry):
        begin, hit = carry
        return begin + seg_len[k], jnp.where(tokens == begin, 1, hit)

    _, opening = lax.fori_loop(
        0, segments, opens, (jnp.int32(0), jnp.zeros((tiles, SPAN), jnp.int32))
    )

    @pl.when(flat > 0)
    def _():
        edge_copy.wait_recv()
        mel_f[0:8, :] = edge[...].astype(F32)[TAIL - 8 :, :]

    left = jnp.where(opening > 0, 0.0, mel_f[pl.ds(7, tiles, stride=2), :])
    stacked = jnp.concatenate(
        [left, mel_f[pl.ds(8, tiles, stride=2), :], mel_f[pl.ds(9, tiles, stride=2), :]], axis=1
    ).astype(BF16)
    channels = conv_w.shape[1]
    for n in range(0, channels, 256):
        summed = (
            jnp.dot(stacked, conv_w[:, n : n + 256], preferred_element_type=F32)
            + jnp.concatenate(
                [bias[k : k + 1, :] for k in range(n // SPAN, (n + 256) // SPAN)], axis=1
            )
        )
        feat[:, n : n + 256] = (
            0.5 * summed * (1.0 + lax.erf(summed * (0.5**0.5)))
        ).astype(BF16)

    def enc_copy(b):
        return pltpu.make_async_remote_copy(
            src_ref=sent.at[b],
            dst_ref=wide.at[pl.ds(pl.multiple_of(FRONT + e * tiles, TAIL), tiles)],
            send_sem=enc_send.at[b],
            recv_sem=enc_recv.at[e],
            device_id={"enc": b},
            device_id_type=MESH,
        )

    fronts = {}
    backs = {}
    for t in range(encs):
        low = max(t * tiles, share - FRONT)
        if low < (t + 1) * tiles:
            fronts[t] = (low - t * tiles, (t + 1) * tiles - low, low - (share - FRONT))
        high = min((t + 1) * tiles, DRIFT)
        if high > t * tiles:
            backs[t] = (0, high - t * tiles, FRONT + share + t * tiles)

    def halo_copy(t, b, plan, send_sem, recv_sem, by):
        begin, count, place = plan[t]
        return pltpu.make_async_remote_copy(
            src_ref=sent.at[b, pl.ds(begin, count)],
            dst_ref=wide.at[pl.ds(place, count)],
            send_sem=send_sem.at[b],
            recv_sem=recv_sem.at[t],
            device_id={"seq": s + by, "enc": b},
            device_id_type=MESH,
        )

    def front_copy(t, b):
        return halo_copy(t, b, fronts, front_send, front_recv, 1)

    def back_copy(t, b):
        return halo_copy(t, b, backs, back_send, back_recv, -1)

    def project(j, carry):
        b = lax.rem(e + encs // 2 + j, encs)
        block = jnp.dot(feat[...], proj[b], preferred_element_type=F32).astype(BF16)
        sent[b] = block

        @pl.when(b != e)
        def _():
            enc_copy(b).start()

        @pl.when(b == e)
        def _():
            wide[pl.ds(pl.multiple_of(FRONT + e * tiles, TAIL), tiles), :] = block

        for t in fronts:

            @pl.when((e == t) & (s < owners - 1))
            def _(t=t):
                front_copy(t, b).start()

        for t in backs:

            @pl.when((e == t) & (s > 0))
            def _(t=t):
                back_copy(t, b).start()

        return carry

    lax.fori_loop(0, encs, project, 0)

    low_half = lane_ids < HDIM

    def block_rows(c):
        return pl.ds(pl.multiple_of(c * SPAN, SPAN), SPAN)

    def head_rows(c):
        return pl.ds(pl.multiple_of(c * 8, 8), 8)

    def spread(columns):
        return jnp.concatenate(
            [
                jnp.where(low_half, columns[:, 2 * i : 2 * i + 1], columns[:, 2 * i + 1 : 2 * i + 2])
                for i in range(halves)
            ],
            axis=1,
        )

    def make_weights(c, carry):
        both = lax.dot_general(
            c_map[block_rows(c), :],
            b_map[block_rows(c), :],
            (((1,), (1,)), ((), ())),
            preferred_element_type=F32,
        )
        run = run_s[head_rows(c), :]
        steps = step_s[head_rows(c), :]
        columns = jnp.transpose(run)
        for h in range(heads):
            gap = columns[:, h : h + 1] - run[h : h + 1, :]
            decay = jnp.exp(jnp.where(row_ids >= lane_ids, gap, -1e30))
            weights[c, h * SPAN : (h + 1) * SPAN, :] = (
                decay * both * steps[h : h + 1, :]
            ).astype(BF16)
        run_wide = spread(columns)
        last = run_wide[SPAN - 1 : SPAN, :]
        grown[block_rows(c), :] = jnp.exp(run_wide)
        tails[block_rows(c), :] = spread(jnp.transpose(steps)) * jnp.exp(last - run_wide)
        lasts[c] = last
        return carry

    lax.fori_loop(0, blocks, make_weights, 0, unroll=4)

    def start_of(last):
        return lax.fori_loop(0, last, lambda k, total: total + seg_len[k], jnp.int32(0))

    for j in range(1, encs):
        peer = lax.rem(e + j, encs)
        pltpu.make_async_remote_copy(
            src_ref=sent.at[peer],
            dst_ref=wide.at[pl.ds(pl.multiple_of(FRONT + peer * tiles, TAIL), tiles)],
            send_sem=enc_send.at[peer],
            recv_sem=enc_recv.at[peer],
            device_id={"enc": peer},
            device_id_type=MESH,
        ).wait_recv()

    @pl.when(s > 0)
    def _():
        tail_copy.wait_recv()
        for t in fronts:
            front_copy(t, 0).wait_recv()

    @pl.when(s < owners - 1)
    def _():
        for t in backs:
            back_copy(t, 0).wait_recv()

    @pl.when(s == 0)
    def _():
        wide[0:FRONT, :] = jnp.zeros((FRONT, width), BF16)
        text_tail[...] = jnp.zeros_like(text_tail)

    @pl.when(s == owners - 1)
    def _():
        wide[FRONT + share : FRONT + share + DRIFT, :] = jnp.zeros((DRIFT, width), BF16)

    held = wide.shape[0]
    spare = held - FRONT - share - DRIFT
    if spare:
        wide[held - spare :, :] = jnp.zeros((spare, width), BF16)

    def segment(k):
        return seg_off[k] - s * rows, seg_len[k], start_of(k) - s * share + FRONT

    def placed(first, count, parts, text_rows):
        ids = lax.broadcasted_iota(jnp.int32, (count, SPAN), 0)
        gaps = lax.broadcasted_iota(jnp.int32, (count, SPAN), 1) - ids
        here = first + ids
        shift = jnp.full((count, SPAN), -(1 << 30), jnp.int32)
        for offset, length, start in parts:
            inside = (here >= offset) & (here < offset + length)
            shift = jnp.where(inside, first - offset + start, shift)
        picks = jnp.concatenate(
            [
                jnp.where(gaps == shift - k, 1.0, 0.0).astype(BF16)
                for k in range(0, held, SPAN)
            ],
            axis=1,
        )
        audio = jnp.dot(picks, wide[...], preferred_element_type=F32)
        is_text = jnp.concatenate([shift] * halves, axis=1) < -(1 << 29)
        return jnp.where(is_text, text_rows, audio)

    own = [segment(2 * s), segment(2 * s + 1)]
    prior = 2 * lax.rem(s + owners - 1, owners)
    earlier = [segment(prior), segment(prior + 1)]
    past = placed(-TAIL, TAIL, earlier, text_tail[...].astype(F32))
    x_rows[0:8, :] = jnp.where(s > 0, past[TAIL - 8 :, :], 0.0)
    state[...] = jnp.zeros_like(state)

    def fill(c, carry):
        first = c * PLACED
        x_rows[pl.ds(pl.multiple_of(first + 8, 8), PLACED), :] = placed(
            first,
            PLACED,
            own,
            text[pl.ds(pl.multiple_of(first, PLACED), PLACED), :].astype(F32),
        )
        return carry

    lax.fori_loop(0, rows // PLACED, fill, 0, unroll=2)

    def place(c, before):
        first = c * SPAN
        near = x_rows[pl.ds(pl.multiple_of(first, 8), SPAN + 8), :]
        summed = near[5 : 5 + SPAN] * taps[0:1, :]
        for j in range(1, 4):
            summed = summed + near[5 + j : 5 + j + SPAN] * taps[j : j + 1, :]
        mixed = (summed / (1.0 + jnp.exp(-summed))).astype(BF16)
        xconv[block_rows(c), :] = mixed
        last = lasts[c]
        inputs = (mixed.astype(F32) * tails[block_rows(c), :]).astype(BF16)
        added = lax.dot_general(
            b_map[block_rows(c), :], inputs, (((0,), (0,)), ((), ())), preferred_element_type=F32
        )
        now = state[...]
        starts[c] = now.astype(BF16)
        before_s[c] = jnp.exp(before)
        state[...] = now * jnp.exp(last) + added
        return before + last

    total = lax.fori_loop(0, blocks, place, jnp.zeros((1, width), F32), unroll=4)

    mine[...] = state[...].astype(BF16)
    mine_total[...] = jnp.broadcast_to(total, mine_total.shape)

    def state_copies(to, slot):
        return (
            pltpu.make_async_remote_copy(
                src_ref=mine,
                dst_ref=states.at[slot],
                send_sem=state_send.at[to],
                recv_sem=state_recv.at[slot],
                device_id={"seq": to},
                device_id_type=MESH,
            ),
            pltpu.make_async_remote_copy(
                src_ref=mine_total,
                dst_ref=totals.at[slot],
                send_sem=total_send.at[to],
                recv_sem=total_recv.at[slot],
                device_id={"seq": to},
                device_id_type=MESH,
            ),
        )

    def send_state(to, carry):
        for copy in state_copies(to, s):
            copy.start()
        return carry

    lax.fori_loop(s + 1, owners, send_state, 0)

    skip = jnp.concatenate(
        [
            jnp.where(low_half[0:1, :], skip_gain[2 * i], skip_gain[2 * i + 1])
            for i in range(halves)
        ],
        axis=1,
    )

    def inner(c, carry):
        mixed = xconv[block_rows(c), :]
        wide_y = jnp.dot(weights[c], mixed, preferred_element_type=F32)
        within = jnp.concatenate(
            [
                jnp.where(
                    low_half,
                    wide_y[2 * i * SPAN : (2 * i + 1) * SPAN, i * SPAN : (i + 1) * SPAN],
                    wide_y[(2 * i + 1) * SPAN : (2 * i + 2) * SPAN, i * SPAN : (i + 1) * SPAN],
                )
                for i in range(halves)
            ],
            axis=1,
        )
        carried = jnp.dot(c_map[block_rows(c), :], starts[c], preferred_element_type=F32)
        y_s[block_rows(c), :] = (
            within + carried * grown[block_rows(c), :] + skip * mixed.astype(F32)
        )
        return carry

    lax.fori_loop(0, blocks, inner, 0, unroll=4)

    state[...] = jnp.zeros_like(state)

    def join(r, carry):
        for copy in state_copies(s, r):
            copy.wait_recv()
        state[...] = state[...] * jnp.exp(totals[r][0:1, :]) + states[r].astype(F32)
        return carry

    lax.fori_loop(0, s, join, 0)
    incoming = state[...].astype(BF16)

    def finish(c, carry):
        carried = jnp.dot(c_map[block_rows(c), :], incoming, preferred_element_type=F32)
        out[block_rows(c), :] = (
            y_s[block_rows(c), :] + carried * before_s[c] * grown[block_rows(c), :]
        ).astype(BF16)
        return carry

    lax.fori_loop(0, blocks, finish, 0, unroll=8)

    @pl.when(flat < owners * encs - 1)
    def _():
        edge_copy.wait_send()

    @pl.when(s < owners - 1)
    def _():
        tail_copy.wait_send()

    for j in range(1, encs):
        enc_copy(lax.rem(e + j, encs)).wait_send()

    for b in range(encs):
        for t in fronts:

            @pl.when((e == t) & (s < owners - 1))
            def _(t=t, b=b):
                front_copy(t, b).wait_send()

        for t in backs:

            @pl.when((e == t) & (s > 0))
            def _(t=t, b=b):
                back_copy(t, b).wait_send()

    def sent_state(to, carry):
        for copy in state_copies(to, s):
            copy.wait_send()
        return carry

    lax.fori_loop(s + 1, owners, sent_state, 0)


def shards(
    mel_frames,
    conv_weight,
    conv_bias,
    projector,
    seg_offsets,
    seg_lengths,
    text_embed,
    mix_taps,
    input_map,
    output_map,
    step_size,
    decay_log,
    skip_gain,
):
    owners = lax.axis_size("seq")
    encs = lax.axis_size("enc")
    frames, mels = mel_frames.shape
    tiles = frames // 2
    channels = conv_weight.shape[1]
    rows, width = text_embed.shape
    heads = step_size.shape[0]
    blocks = rows // SPAN
    states = input_map.shape[1]
    held = -(-(FRONT + encs * tiles + DRIFT) // SPAN) * SPAN
    vmem = pl.BlockSpec(memory_space=pltpu.VMEM)
    smem = pl.BlockSpec(memory_space=pltpu.SMEM)
    dma = pltpu.SemaphoreType.DMA
    return pl.pallas_call(
        functools.partial(kernel, owners, encs),
        out_shape=jax.ShapeDtypeStruct((rows, width), BF16),
        in_specs=[smem, smem] + [vmem] * 9 + [smem, smem],
        out_specs=vmem,
        scratch_shapes=[
            pltpu.VMEM((8 + frames, mels), F32),
            pltpu.VMEM((TAIL, mels), BF16),
            pltpu.VMEM((TAIL, width), BF16),
            pltpu.VMEM((tiles, channels), BF16),
            pltpu.VMEM((encs, tiles, width), BF16),
            pltpu.VMEM((held, width), BF16),
            pltpu.VMEM((rows + 8, width), F32),
            pltpu.VMEM((rows, width), BF16),
            pltpu.VMEM((blocks * 8, SPAN), F32),
            pltpu.VMEM((blocks * 8, SPAN), F32),
            pltpu.VMEM((blocks, heads * SPAN, SPAN), BF16),
            pltpu.VMEM((rows, width), F32),
            pltpu.VMEM((rows, width), F32),
            pltpu.VMEM((states, width), F32),
            pltpu.VMEM((blocks, states, width), BF16),
            pltpu.VMEM((blocks, 1, width), F32),
            pltpu.VMEM((blocks, 1, width), F32),
            pltpu.VMEM((rows, width), F32),
            pltpu.VMEM((states, width), BF16),
            pltpu.VMEM((8, width), F32),
            pltpu.VMEM((owners, states, width), BF16),
            pltpu.VMEM((owners, 8, width), F32),
            dma((2,)),
            dma((2,)),
            dma((encs,)),
            dma((encs,)),
            dma((encs,)),
            dma((encs,)),
            dma((encs,)),
            dma((encs,)),
            dma((owners,)),
            dma((owners,)),
            dma((owners,)),
            dma((owners,)),
        ],
        compiler_params=pltpu.CompilerParams(
            collective_id=0, has_side_effects=True, vmem_limit_bytes=48 * 1024 * 1024
        ),
    )(
        seg_offsets,
        seg_lengths,
        mel_frames,
        conv_weight,
        conv_bias.reshape(channels // SPAN, SPAN),
        jnp.transpose(projector, (1, 0, 2)),
        text_embed,
        mix_taps,
        input_map,
        output_map,
        step_size,
        decay_log,
        skip_gain,
    )


def solution(mesh):
    return jax.shard_map(
        shards,
        mesh=mesh,
        in_specs=(
            P(("seq", "enc"), None),
            P(),
            P(),
            P(None, None, "head"),
            P(),
            P(),
            P("seq", ("enc", "head")),
            P(None, ("enc", "head")),
            P("seq", "enc"),
            P("seq", "enc"),
            P(("enc", "head"), "seq"),
            P(("enc", "head")),
            P(("enc", "head")),
        ),
        out_specs=P("seq", ("enc", "head")),
        check_vma=False,
    )
```

```python
import functools

import jax
import jax.numpy as jnp
from jax import lax
from jax.experimental import pallas as pl
from jax.experimental.pallas import tpu as pltpu
from jax.sharding import PartitionSpec as P

HDIM = 64
SPAN = 128
DRIFT = 256
TAIL = 16
PLACED = 256
FRONT = DRIFT + TAIL
MESH = pl.DeviceIdType.MESH
F32 = jnp.float32
BF16 = jnp.bfloat16


def kernel(
    owners,
    encs,
    seg_off,
    seg_len,
    mel,
    conv_w,
    bias,
    proj,
    text,
    taps,
    b_map,
    c_map,
    step,
    decay_log,
    skip_gain,
    out,
    mel_f,
    edge,
    text_tail,
    feat,
    sent,
    wide,
    x_rows,
    xconv,
    step_s,
    run_s,
    weights,
    grown,
    tails,
    state,
    starts,
    before_s,
    lasts,
    y_s,
    mine,
    mine_total,
    states,
    totals,
    edge_sems,
    tail_sems,
    enc_send,
    enc_recv,
    front_send,
    front_recv,
    back_send,
    back_recv,
    state_send,
    state_recv,
    total_send,
    total_recv,
):
    s = lax.axis_index("seq")
    e = lax.axis_index("enc")
    frames = mel.shape[0]
    tiles = frames // 2
    share = encs * tiles
    rows, width = text.shape
    blocks = rows // SPAN
    heads = step.shape[0]
    halves = width // SPAN
    flat = s * encs + e
    segments = seg_off.shape[0]

    barrier = pltpu.get_barrier_semaphore()

    def greet(device):
        pl.semaphore_signal(barrier, inc=1, device_id=device, device_id_type=MESH)

    for j in range(1, encs):
        greet({"enc": lax.rem(e + j, encs)})

    @pl.when(s > 0)
    def _():
        for j in range(encs):
            greet({"seq": s - 1, "enc": j})

    @pl.when(s < owners - 1)
    def _():
        for j in range(encs):
            greet({"seq": s + 1, "enc": j})

    def greet_far(r, carry):
        @pl.when((r > s + 1) | (r < s - 1))
        def _():
            greet({"seq": r})

        return carry

    lax.fori_loop(0, owners, greet_far, 0)
    beside = (s > 0).astype(jnp.int32) + (s < owners - 1).astype(jnp.int32)
    pl.semaphore_wait(barrier, encs - 1 + beside * encs + owners - 1 - beside)

    edge_copy = pltpu.make_async_remote_copy(
        src_ref=mel.at[pl.ds(frames - TAIL, TAIL)],
        dst_ref=edge,
        send_sem=edge_sems.at[0],
        recv_sem=edge_sems.at[1],
        device_id={"seq": (flat + 1) // encs, "enc": lax.rem(e + 1, encs)},
        device_id_type=MESH,
    )
    tail_copy = pltpu.make_async_remote_copy(
        src_ref=text.at[pl.ds(rows - TAIL, TAIL)],
        dst_ref=text_tail,
        send_sem=tail_sems.at[0],
        recv_sem=tail_sems.at[1],
        device_id={"seq": s + 1},
        device_id_type=MESH,
    )

    @pl.when(flat < owners * encs - 1)
    def _():
        edge_copy.start()

    @pl.when(s < owners - 1)
    def _():
        tail_copy.start()

    step_s[...] = jnp.zeros_like(step_s)
    for c in range(blocks):
        step_s[c * 8 : c * 8 + heads, :] = step[:, c * SPAN : (c + 1) * SPAN]
    head_ids = lax.broadcasted_iota(jnp.int32, (8, SPAN), 0)
    rate = jnp.zeros((8, SPAN), F32)
    for h in range(heads):
        rate = jnp.where(head_ids == h, jnp.exp(jnp.full((8, SPAN), decay_log[h], F32)), rate)
    logs = -(step_s[...].reshape(blocks, 8, SPAN) * rate[None]).reshape(blocks * 8, SPAN)
    row_ids = lax.broadcasted_iota(jnp.int32, (SPAN, SPAN), 0)
    lane_ids = lax.broadcasted_iota(jnp.int32, (SPAN, SPAN), 1)
    upper = (row_ids <= lane_ids).astype(F32)
    run_s[...] = jnp.dot(
        logs, upper, preferred_element_type=F32, precision=lax.Precision.HIGHEST
    )

    mel_f[8:, :] = mel[...].astype(F32)

    @pl.when(flat == 0)
    def _():
        mel_f[0:8, :] = jnp.zeros((8, mel.shape[1]), F32)

    tokens = flat * tiles + lax.broadcasted_iota(jnp.int32, (tiles, SPAN), 0)

    def opens(k, carry):
        begin, hit = carry
        return begin + seg_len[k], jnp.where(tokens == begin, 1, hit)

    _, opening = lax.fori_loop(
        0, segments, opens, (jnp.int32(0), jnp.zeros((tiles, SPAN), jnp.int32))
    )

    @pl.when(flat > 0)
    def _():
        edge_copy.wait_recv()
        mel_f[0:8, :] = edge[...].astype(F32)[TAIL - 8 :, :]

    left = jnp.where(opening > 0, 0.0, mel_f[pl.ds(7, tiles, stride=2), :])
    stacked = jnp.concatenate(
        [left, mel_f[pl.ds(8, tiles, stride=2), :], mel_f[pl.ds(9, tiles, stride=2), :]], axis=1
    ).astype(BF16)
    channels = conv_w.shape[1]
    for n in range(0, channels, 256):
        summed = (
            jnp.dot(stacked, conv_w[:, n : n + 256], preferred_element_type=F32)
            + jnp.concatenate(
                [bias[k : k + 1, :] for k in range(n // SPAN, (n + 256) // SPAN)], axis=1
            )
        )
        feat[:, n : n + 256] = (
            0.5 * summed * (1.0 + lax.erf(summed * (0.5**0.5)))
        ).astype(BF16)

    def enc_copy(b):
        return pltpu.make_async_remote_copy(
            src_ref=sent.at[b],
            dst_ref=wide.at[pl.ds(pl.multiple_of(FRONT + e * tiles, TAIL), tiles)],
            send_sem=enc_send.at[b],
            recv_sem=enc_recv.at[e],
            device_id={"enc": b},
            device_id_type=MESH,
        )

    fronts = {}
    backs = {}
    for t in range(encs):
        low = max(t * tiles, share - FRONT)
        if low < (t + 1) * tiles:
            fronts[t] = (low - t * tiles, (t + 1) * tiles - low, low - (share - FRONT))
        high = min((t + 1) * tiles, DRIFT)
        if high > t * tiles:
            backs[t] = (0, high - t * tiles, FRONT + share + t * tiles)

    def halo_copy(t, b, plan, send_sem, recv_sem, by):
        begin, count, place = plan[t]
        return pltpu.make_async_remote_copy(
            src_ref=sent.at[b, pl.ds(begin, count)],
            dst_ref=wide.at[pl.ds(place, count)],
            send_sem=send_sem.at[b],
            recv_sem=recv_sem.at[t],
            device_id={"seq": s + by, "enc": b},
            device_id_type=MESH,
        )

    def front_copy(t, b):
        return halo_copy(t, b, fronts, front_send, front_recv, 1)

    def back_copy(t, b):
        return halo_copy(t, b, backs, back_send, back_recv, -1)

    def project(j, carry):
        b = lax.rem(e + j, encs)
        block = jnp.dot(feat[...], proj[b], preferred_element_type=F32).astype(BF16)
        sent[b] = block

        @pl.when(b != e)
        def _():
            enc_copy(b).start()

        @pl.when(b == e)
        def _():
            wide[pl.ds(pl.multiple_of(FRONT + e * tiles, TAIL), tiles), :] = block

        for t in fronts:

            @pl.when((e == t) & (s < owners - 1))
            def _(t=t):
                front_copy(t, b).start()

        for t in backs:

            @pl.when((e == t) & (s > 0))
            def _(t=t):
                back_copy(t, b).start()

        return carry

    order = sorted(range(1, encs), key=lambda j: (j < encs // 2, j)) + [0]
    for j in order:
        project(j, 0)

    low_half = lane_ids < HDIM

    def block_rows(c):
        return pl.ds(pl.multiple_of(c * SPAN, SPAN), SPAN)

    def head_rows(c):
        return pl.ds(pl.multiple_of(c * 8, 8), 8)

    def spread(columns):
        return jnp.concatenate(
            [
                jnp.where(low_half, columns[:, 2 * i : 2 * i + 1], columns[:, 2 * i + 1 : 2 * i + 2])
                for i in range(halves)
            ],
            axis=1,
        )

    def make_weights(c, carry):
        both = lax.dot_general(
            c_map[block_rows(c), :],
            b_map[block_rows(c), :],
            (((1,), (1,)), ((), ())),
            preferred_element_type=F32,
        )
        run = run_s[head_rows(c), :]
        steps = step_s[head_rows(c), :]
        columns = jnp.transpose(run)
        for h in range(heads):
            gap = columns[:, h : h + 1] - run[h : h + 1, :]
            decay = jnp.exp(jnp.where(row_ids >= lane_ids, gap, -1e30))
            weights[c, h * SPAN : (h + 1) * SPAN, :] = (
                decay * both * steps[h : h + 1, :]
            ).astype(BF16)
        run_wide = spread(columns)
        last = run_wide[SPAN - 1 : SPAN, :]
        grown[block_rows(c), :] = jnp.exp(run_wide)
        tails[block_rows(c), :] = spread(jnp.transpose(steps)) * jnp.exp(last - run_wide)
        lasts[c] = last
        return carry

    lax.fori_loop(0, blocks, make_weights, 0, unroll=8)

    def start_of(last):
        return lax.fori_loop(0, last, lambda k, total: total + seg_len[k], jnp.int32(0))

    for j in range(1, encs):
        peer = lax.rem(e + j, encs)
        pltpu.make_async_remote_copy(
            src_ref=sent.at[peer],
            dst_ref=wide.at[pl.ds(pl.multiple_of(FRONT + peer * tiles, TAIL), tiles)],
            send_sem=enc_send.at[peer],
            recv_sem=enc_recv.at[peer],
            device_id={"enc": peer},
            device_id_type=MESH,
        ).wait_recv()

    @pl.when(s > 0)
    def _():
        tail_copy.wait_recv()
        for t in fronts:
            front_copy(t, 0).wait_recv()

    @pl.when(s < owners - 1)
    def _():
        for t in backs:
            back_copy(t, 0).wait_recv()

    @pl.when(s == 0)
    def _():
        wide[0:FRONT, :] = jnp.zeros((FRONT, width), BF16)
        text_tail[...] = jnp.zeros_like(text_tail)

    @pl.when(s == owners - 1)
    def _():
        wide[FRONT + share : FRONT + share + DRIFT, :] = jnp.zeros((DRIFT, width), BF16)

    held = wide.shape[0]
    spare = held - FRONT - share - DRIFT
    if spare:
        wide[held - spare :, :] = jnp.zeros((spare, width), BF16)

    def segment(k):
        return seg_off[k] - s * rows, seg_len[k], start_of(k) - s * share + FRONT

    def placed(first, count, parts, text_rows):
        ids = lax.broadcasted_iota(jnp.int32, (count, SPAN), 0)
        gaps = lax.broadcasted_iota(jnp.int32, (count, SPAN), 1) - ids
        here = first + ids
        shift = jnp.full((count, SPAN), -(1 << 30), jnp.int32)
        for offset, length, start in parts:
            inside = (here >= offset) & (here < offset + length)
            shift = jnp.where(inside, first - offset + start, shift)
        picks = jnp.concatenate(
            [
                jnp.where(gaps == shift - k, 1.0, 0.0).astype(BF16)
                for k in range(0, held, SPAN)
            ],
            axis=1,
        )
        audio = jnp.dot(picks, wide[...], preferred_element_type=F32)
        is_text = jnp.concatenate([shift] * halves, axis=1) < -(1 << 29)
        return jnp.where(is_text, text_rows, audio)

    own = [segment(2 * s), segment(2 * s + 1)]
    prior = 2 * lax.rem(s + owners - 1, owners)
    earlier = [segment(prior), segment(prior + 1)]
    past = placed(-TAIL, TAIL, earlier, text_tail[...].astype(F32))
    x_rows[0:8, :] = jnp.where(s > 0, past[TAIL - 8 :, :], 0.0)
    state[...] = jnp.zeros_like(state)

    def fill(c, carry):
        first = c * PLACED
        x_rows[pl.ds(pl.multiple_of(first + 8, 8), PLACED), :] = placed(
            first,
            PLACED,
            own,
            text[pl.ds(pl.multiple_of(first, PLACED), PLACED), :].astype(F32),
        )
        return carry

    lax.fori_loop(0, rows // PLACED, fill, 0, unroll=4)

    def place(c, before):
        first = c * SPAN
        near = x_rows[pl.ds(pl.multiple_of(first, 8), SPAN + 8), :]
        summed = near[5 : 5 + SPAN] * taps[0:1, :]
        for j in range(1, 4):
            summed = summed + near[5 + j : 5 + j + SPAN] * taps[j : j + 1, :]
        mixed = (summed / (1.0 + jnp.exp(-summed))).astype(BF16)
        xconv[block_rows(c), :] = mixed
        last = lasts[c]
        inputs = (mixed.astype(F32) * tails[block_rows(c), :]).astype(BF16)
        added = lax.dot_general(
            b_map[block_rows(c), :], inputs, (((0,), (0,)), ((), ())), preferred_element_type=F32
        )
        now = state[...]
        starts[c] = now.astype(BF16)
        before_s[c] = jnp.exp(before)
        state[...] = now * jnp.exp(last) + added
        return before + last

    total = lax.fori_loop(0, blocks, place, jnp.zeros((1, width), F32), unroll=4)

    mine[...] = state[...].astype(BF16)
    mine_total[...] = jnp.broadcast_to(total, mine_total.shape)

    def state_copies(to, slot):
        return (
            pltpu.make_async_remote_copy(
                src_ref=mine,
                dst_ref=states.at[slot],
                send_sem=state_send.at[to],
                recv_sem=state_recv.at[slot],
                device_id={"seq": to},
                device_id_type=MESH,
            ),
            pltpu.make_async_remote_copy(
                src_ref=mine_total,
                dst_ref=totals.at[slot],
                send_sem=total_send.at[to],
                recv_sem=total_recv.at[slot],
                device_id={"seq": to},
                device_id_type=MESH,
            ),
        )

    def send_state(to, carry):
        for copy in state_copies(to, s):
            copy.start()
        return carry

    lax.fori_loop(s + 1, owners, send_state, 0)

    skip = jnp.concatenate(
        [
            jnp.where(low_half[0:1, :], skip_gain[2 * i], skip_gain[2 * i + 1])
            for i in range(halves)
        ],
        axis=1,
    )

    def inner(c, carry):
        mixed = xconv[block_rows(c), :]
        wide_y = jnp.dot(weights[c], mixed, preferred_element_type=F32)
        within = jnp.concatenate(
            [
                jnp.where(
                    low_half,
                    wide_y[2 * i * SPAN : (2 * i + 1) * SPAN, i * SPAN : (i + 1) * SPAN],
                    wide_y[(2 * i + 1) * SPAN : (2 * i + 2) * SPAN, i * SPAN : (i + 1) * SPAN],
                )
                for i in range(halves)
            ],
            axis=1,
        )
        carried = jnp.dot(c_map[block_rows(c), :], starts[c], preferred_element_type=F32)
        y_s[block_rows(c), :] = (
            within + carried * grown[block_rows(c), :] + skip * mixed.astype(F32)
        )
        return carry

    lax.fori_loop(0, blocks, inner, 0, unroll=4)

    state[...] = jnp.zeros_like(state)

    def join(r, carry):
        for copy in state_copies(s, r):
            copy.wait_recv()
        state[...] = state[...] * jnp.exp(totals[r][0:1, :]) + states[r].astype(F32)
        return carry

    lax.fori_loop(0, s, join, 0)
    incoming = state[...].astype(BF16)

    def finish(c, carry):
        carried = jnp.dot(c_map[block_rows(c), :], incoming, preferred_element_type=F32)
        out[block_rows(c), :] = (
            y_s[block_rows(c), :] + carried * before_s[c] * grown[block_rows(c), :]
        ).astype(BF16)
        return carry

    lax.fori_loop(0, blocks, finish, 0, unroll=8)

    @pl.when(flat < owners * encs - 1)
    def _():
        edge_copy.wait_send()

    @pl.when(s < owners - 1)
    def _():
        tail_copy.wait_send()

    for j in range(1, encs):
        enc_copy(lax.rem(e + j, encs)).wait_send()

    for b in range(encs):
        for t in fronts:

            @pl.when((e == t) & (s < owners - 1))
            def _(t=t, b=b):
                front_copy(t, b).wait_send()

        for t in backs:

            @pl.when((e == t) & (s > 0))
            def _(t=t, b=b):
                back_copy(t, b).wait_send()

    def sent_state(to, carry):
        for copy in state_copies(to, s):
            copy.wait_send()
        return carry

    lax.fori_loop(s + 1, owners, sent_state, 0)


def shards(
    mel_frames,
    conv_weight,
    conv_bias,
    projector,
    seg_offsets,
    seg_lengths,
    text_embed,
    mix_taps,
    input_map,
    output_map,
    step_size,
    decay_log,
    skip_gain,
):
    owners = lax.axis_size("seq")
    encs = lax.axis_size("enc")
    frames, mels = mel_frames.shape
    tiles = frames // 2
    channels = conv_weight.shape[1]
    rows, width = text_embed.shape
    heads = step_size.shape[0]
    blocks = rows // SPAN
    states = input_map.shape[1]
    held = -(-(FRONT + encs * tiles + DRIFT) // SPAN) * SPAN
    vmem = pl.BlockSpec(memory_space=pltpu.VMEM)
    smem = pl.BlockSpec(memory_space=pltpu.SMEM)
    dma = pltpu.SemaphoreType.DMA
    return pl.pallas_call(
        functools.partial(kernel, owners, encs),
        out_shape=jax.ShapeDtypeStruct((rows, width), BF16),
        in_specs=[smem, smem] + [vmem] * 9 + [smem, smem],
        out_specs=vmem,
        scratch_shapes=[
            pltpu.VMEM((8 + frames, mels), F32),
            pltpu.VMEM((TAIL, mels), BF16),
            pltpu.VMEM((TAIL, width), BF16),
            pltpu.VMEM((tiles, channels), BF16),
            pltpu.VMEM((encs, tiles, width), BF16),
            pltpu.VMEM((held, width), BF16),
            pltpu.VMEM((rows + 8, width), F32),
            pltpu.VMEM((rows, width), BF16),
            pltpu.VMEM((blocks * 8, SPAN), F32),
            pltpu.VMEM((blocks * 8, SPAN), F32),
            pltpu.VMEM((blocks, heads * SPAN, SPAN), BF16),
            pltpu.VMEM((rows, width), F32),
            pltpu.VMEM((rows, width), F32),
            pltpu.VMEM((states, width), F32),
            pltpu.VMEM((blocks, states, width), BF16),
            pltpu.VMEM((blocks, 1, width), F32),
            pltpu.VMEM((blocks, 1, width), F32),
            pltpu.VMEM((rows, width), F32),
            pltpu.VMEM((states, width), BF16),
            pltpu.VMEM((8, width), F32),
            pltpu.VMEM((owners, states, width), BF16),
            pltpu.VMEM((owners, 8, width), F32),
            dma((2,)),
            dma((2,)),
            dma((encs,)),
            dma((encs,)),
            dma((encs,)),
            dma((encs,)),
            dma((encs,)),
            dma((encs,)),
            dma((owners,)),
            dma((owners,)),
            dma((owners,)),
            dma((owners,)),
        ],
        compiler_params=pltpu.CompilerParams(
            collective_id=0, has_side_effects=True, vmem_limit_bytes=48 * 1024 * 1024
        ),
    )(
        seg_offsets,
        seg_lengths,
        mel_frames,
        conv_weight,
        conv_bias.reshape(channels // SPAN, SPAN),
        jnp.transpose(projector, (1, 0, 2)),
        text_embed,
        mix_taps,
        input_map,
        output_map,
        step_size,
        decay_log,
        skip_gain,
    )


def solution(mesh):
    return jax.shard_map(
        shards,
        mesh=mesh,
        in_specs=(
            P(("seq", "enc"), None),
            P(),
            P(),
            P(None, None, "head"),
            P(),
            P(),
            P("seq", ("enc", "head")),
            P(None, ("enc", "head")),
            P("seq", "enc"),
            P("seq", "enc"),
            P(("enc", "head"), "seq"),
            P(("enc", "head")),
            P(("enc", "head")),
        ),
        out_specs=P("seq", ("enc", "head")),
        check_vma=False,
    )
```
